128 devices in a mesh: grp: 4 (over z), seq: 8 (over y_lo, x), rep: 4 (over y_hi, core).
Axes of the slice: x: 4, y: 4 (y_hi: 2, y_lo: 2; y = y_hi * 2 + y_lo), z: 4, core: 2. Of those that a mesh axis runs over, the one named last changes fastest.
Arguments:
- base_hidden: bfloat16 [32, 192, 3072], P(('seq', 'rep'), 'grp'), may hold values from -6 to 6
- base_query: bfloat16 [32, 192, 3072], P(('seq', 'rep'), 'grp'), may hold values from -24 to 24
- base_key: bfloat16 [32, 192, 3072], P(('seq', 'rep'), 'grp'), may hold values from -24 to 24
- base_value: bfloat16 [32, 192, 3072], P(('seq', 'rep'), 'grp'), may hold values from -6 to 6
- base_text_key: bfloat16 [512, 3072], P(None, 'seq'), may hold values from -6 to 6
- base_text_value: bfloat16 [512, 3072], P(None, 'seq'), may hold values from -24 to 24
- base_out_weight: bfloat16 [3072, 3072], P('seq'), may hold values from -0.109375 to 0.109375
- control_hidden: bfloat16 [6144, 3072], P(('seq', 'rep'), 'grp'), may hold values from -6 to 6
- control_query: bfloat16 [6144, 3072], P(('seq', 'rep'), 'grp'), may hold values from -24 to 24
- control_key: bfloat16 [6144, 3072], P(('seq', 'rep'), 'grp'), may hold values from -24 to 24
- control_value: bfloat16 [6144, 3072], P(('seq', 'rep'), 'grp'), may hold values from -6 to 6
- control_text_key: bfloat16 [512, 3072], P(None, 'grp'), may hold values from -6 to 6
- control_text_value: bfloat16 [512, 3072], P(None, 'grp'), may hold values from -24 to 24
- control_out_weight: bfloat16 [3072, 3072], P('grp'), may hold values from -0.109375 to 0.109375
- gate_table: float32 [28, 2, 3072], replicated, may hold values from 0.3 to 3
- control_gain: float32 [3072], replicated, may hold values from 0.3 to 3
- timestep: int32 [1], replicated, may hold values from 0 to 27
- text_length: int32 [1], replicated, may hold values from 128 to 512
Outputs:
- base_out: bfloat16 [32, 192, 3072], P(('seq', 'rep'), 'grp')
The draws below stay inside these ranges and needn't reach their ends.
All inputs are finite; a program needn't handle non-finite values.
Results may differ from the reference program's by a relative error of at most 0.017.
Values may be sent and summed in bfloat16 or wider, within the bound.
A program may use at most 192 MiB of HBM per device.

```python
import math
import jax
import jax.numpy as jnp
from jax import lax

D = 3072
HEADS = 24
HEAD_DIM = 128
TXT = 512
STEPS = 28
BLOCKS = 32
ROWG = 192
IMG = 6144


def drawn_rows(key):
    return 1.58 * jnp.clip(jax.random.normal(key, (IMG, D), jnp.float32), -6.0, 6.0)


def query_rows(key, salt):
    key = jax.random.fold_in(key, salt + 1)
    result = drawn_rows(key)
    return result


def key_rows(key, salt):
    key = jax.random.fold_in(key, salt + 2)
    result = drawn_rows(key)
    return result


def draw_base_query(key, part):
    return query_rows(key, 101).reshape(BLOCKS, ROWG, D).astype(jnp.bfloat16)


def draw_base_key(key, part):
    return key_rows(key, 101).reshape(BLOCKS, ROWG, D).astype(jnp.bfloat16)


def draw_control_query(key, part):
    return query_rows(key, 211).astype(jnp.bfloat16)


def draw_control_key(key, part):
    return key_rows(key, 211).astype(jnp.bfloat16)


def steps_of(rng, shape, pieces, smallest, largest):
    gain, own = 1.0, jax.random.fold_in(rng, 6)
    for dim, parts in pieces:
        steps = jnp.exp(jax.random.uniform(jax.random.fold_in(own, dim), (parts,), jnp.float32, smallest / len(pieces), largest / len(pieces)))
        gain = gain * jnp.repeat(steps, shape[dim] // parts).reshape([-1 if axis == dim else 1 for axis in range(len(shape))])
    return gain


def bell_draw(own_key, dims, width, limit, cuts=(), held_as=jnp.bfloat16):
    array = width * jax.random.normal(own_key, dims, jnp.float32)
    if cuts:
        array = array * steps_of(own_key, dims, cuts, -0.22, 0.18)
    return jnp.clip(array, -limit, limit).astype(held_as)


def setup_inputs(seed: int = 0) -> dict:
    key_of = jax.random.split(jax.random.key(seed), 19)
    base_hidden = bell_draw(key_of[0], (BLOCKS, ROWG, D), 1.0, 6.0, ((0, 32), (1, 4)))
    base_query = draw_base_query(jax.random.fold_in(key_of[18], 71), 0)
    base_key = draw_base_key(jax.random.fold_in(key_of[18], 71), 0)
    base_value = bell_draw(key_of[3], (BLOCKS, ROWG, D), 1.0, 6.0, ((0, 32), (1, 4)))
    base_text_key = bell_draw(key_of[4], (TXT, D), 2.0, 6.0, ((1, 8),))
    base_text_value = bell_draw(key_of[5], (TXT, D), 4.0, 24.0, ((1, 8),))
    base_out_weight = bell_draw(key_of[6], (D, D), D ** -0.5, 0.109375, ((0, 8),))
    control_hidden = bell_draw(key_of[7], (IMG, D), 1.0, 6.0, ((0, 32), (1, 4)))
    control_query = draw_control_query(jax.random.fold_in(key_of[18], 71), 0)
    control_key = draw_control_key(jax.random.fold_in(key_of[18], 71), 0)
    control_value = bell_draw(key_of[10], (IMG, D), 1.0, 6.0, ((0, 32), (1, 4)))
    control_text_key = bell_draw(key_of[11], (TXT, D), 2.0, 6.0, ((1, 4),))
    control_text_value = bell_draw(key_of[12], (TXT, D), 4.0, 24.0, ((1, 4),))
    control_out_weight = bell_draw(key_of[13], (D, D), D ** -0.5, 0.109375, ((0, 4),))
    gate_table = jnp.clip(jnp.exp(jax.random.uniform(key_of[14], (STEPS, 2, D), jnp.float32, math.log(0.3), math.log(3.0))), 0.3, 3.0)
    control_gain = jnp.clip(jnp.exp(jax.random.uniform(key_of[15], (D,), jnp.float32, math.log(0.3), math.log(3.0))), 0.3, 3.0)
    timestep = jax.random.randint(key_of[16], (1,), 0, STEPS).astype(jnp.int32)
    text_length = jax.random.randint(key_of[17], (1,), TXT // 4, TXT + 1).astype(jnp.int32)
    return dict(base_hidden=base_hidden, base_query=base_query, base_key=base_key, base_value=base_value, base_text_key=base_text_key, base_text_value=base_text_value, base_out_weight=base_out_weight, control_hidden=control_hidden, control_query=control_query, control_key=control_key, control_value=control_value, control_text_key=control_text_key, control_text_value=control_text_value, control_out_weight=control_out_weight, gate_table=gate_table, control_gain=control_gain, timestep=timestep, text_length=text_length)


def attend(queries, image_keys, image_values, text_key, text_value, text_length):
    score_scale = 1.0 / math.sqrt(HEAD_DIM)
    all_keys = jnp.concatenate([text_key, image_keys], 0)
    all_values = jnp.concatenate([text_value, image_values], 0)
    key_valid = jnp.concatenate([lax.iota(jnp.int32, TXT) < text_length[0], jnp.ones((IMG,), dtype=bool)])
    row_count = queries.shape[0]
    head_queries = queries.reshape(row_count, HEADS, HEAD_DIM).transpose(1, 0, 2)
    head_keys = all_keys.reshape(TXT + IMG, HEADS, HEAD_DIM).transpose(1, 0, 2)
    head_values = all_values.reshape(TXT + IMG, HEADS, HEAD_DIM).transpose(1, 0, 2)

    def one_head(operands):
        head_q, head_k, head_v = operands
        scores = jnp.dot(head_q, head_k.T, preferred_element_type=jnp.float32) * score_scale
        scores = jnp.where(key_valid[None, :], scores, -1e+30)
        running_max = lax.optimization_barrier(jnp.max(scores, axis=-1, keepdims=True))
        weights = jnp.exp(scores - running_max)
        denom_sum = lax.optimization_barrier(jnp.sum(weights, axis=-1))
        weighted = jnp.dot(weights.astype(jnp.bfloat16), head_v, preferred_element_type=jnp.float32)
        return (weighted / denom_sum[:, None]).astype(jnp.bfloat16)
    outputs = lax.map(one_head, (head_queries, head_keys, head_values))
    return outputs.transpose(1, 0, 2).reshape(row_count, D)

def reference(base_hidden, base_query, base_key, base_value, base_text_key, base_text_value, base_out_weight, control_hidden, control_query, control_key, control_value, control_text_key, control_text_value, control_out_weight, gate_table, control_gain, timestep, text_length):
    step_gates = gate_table[timestep[0]]
    base_attn = attend(base_query.reshape(IMG, D), base_key.reshape(IMG, D), base_value.reshape(IMG, D), base_text_key, base_text_value, text_length)
    base_proj = jnp.dot(base_attn, base_out_weight, preferred_element_type=jnp.float32)
    control_attn = attend(control_query, control_key, control_value, control_text_key, control_text_value, text_length)
    control_proj = jnp.dot(control_attn, control_out_weight, preferred_element_type=jnp.float32)
    residual = control_gain * (control_hidden.astype(jnp.float32) + step_gates[1] * control_proj)
    mixed = base_hidden.reshape(IMG, D).astype(jnp.float32) + step_gates[0] * base_proj + residual
    return mixed.astype(jnp.bfloat16).reshape(BLOCKS, ROWG, D)
```

```python
import math

import jax
import jax.numpy as jnp
from jax import lax
from jax.experimental import pallas as pl
from jax.experimental.pallas import tpu as pltpu
from jax.sharding import PartitionSpec as P

HD = 128
NH = 3
OWN = 768
TXH = 256
NB = OWN // 192
KA = TXH + 2 * OWN
KALL = TXH + 4 * OWN
ROWS = 384
CH = 768
C2 = math.log2(math.e) / math.sqrt(HD)
NT = (((1,), (1,)), ((), ()))
MESH = pl.DeviceIdType.MESH


def remote(src, dst, ssem, rsem, dev):
    return pltpu.make_async_remote_copy(
        src_ref=src, dst_ref=dst, send_sem=ssem, recv_sem=rsem, device_id=dev, device_id_type=MESH
    )


def wait_bytes(ref, sem):
    pltpu.make_async_copy(ref, ref, sem).wait()


def kernel(
    tl, bh, bq, bk, bv, btk, btv, wb, ch, cq, ck, cv, ctk, ctv, wc, gates, gain, out,
    Q, K, V, M, L, A, PO, PS, RO, RS, O, OG, WX, WC, HID, SB, SC, RB, RC,
    s1_recv, s1_base, s1_ctl, ex_send, ex_recv, q_send, q_recv, p_send, p_recv,
    g_send, g_recv, w_send, w_recv, r_send, r_recv, loc,
):
    z = lax.axis_index("grp")
    seq = lax.axis_index("seq")
    rep = lax.axis_index("rep")
    x, yl = lax.rem(seq, 4), seq // 4
    yh, c = rep // 2, lax.rem(rep, 2)
    y = yh * 2 + yl

    def dev(xx, yy, zz, cc):
        return {"grp": zz, "seq": lax.rem(yy, 2) * 4 + xx, "rep": (yy // 2) * 2 + cc}

    sib = dev(x, y, z, 1 - c)
    pos = (1 - yh) * z + yh * x
    pa = pos + 1 - 2 * lax.rem(pos, 2)
    pb = lax.rem(pos + 3 - 2 * lax.rem(pos, 2), 4)
    dev_a = dev(yh * pa + (1 - yh) * x, y, (1 - yh) * pa + yh * z, c)
    dev_b = dev(yh * pb + (1 - yh) * x, y, (1 - yh) * pb + yh * z, c)
    thalf = pos // 2

    w_loc = [
        pltpu.make_async_copy(wc, WC, loc.at[0]),
        pltpu.make_async_copy(wb, WX.at[pl.ds(pl.multiple_of(yl * 384, 128), 384)], loc.at[1]),
        pltpu.make_async_copy(ch, HID, loc.at[2]),
    ]

    def text_copies(h, is_base):
        rows = pl.ds(pl.multiple_of(thalf * TXH, TXH), TXH)
        if is_base:
            cols = pl.ds(h * HD, HD)
            srcs = (btk, btv)
        else:
            cols = pl.ds(pl.multiple_of(yl * 384 + h * HD, HD), HD)
            srcs = (ctk, ctv)
        return [
            pltpu.make_async_copy(srcs[i].at[rows, cols], (K, V)[i].at[h, pl.ds(0, TXH)], loc.at[3 + i * NH + h])
            for i in range(2)
        ]

    @pl.when(yh == 0)
    def _():
        for h in range(NH):
            for cp in text_copies(h, True):
                cp.start()

    @pl.when(yh == 1)
    def _():
        for h in range(NH):
            for cp in text_copies(h, False):
                cp.start()

    barrier = pltpu.get_barrier_semaphore()
    peers = [dev(lax.rem(x + i % 4, 4), lax.rem(y + i // 4, 4), z, c) for i in range(1, 16)]
    peers += [dev(x, y, lax.rem(z + i, 4), c) for i in range(1, 4)] + [sib]
    for d in peers:
        pl.semaphore_signal(barrier, inc=1, device_id=d, device_id_type=MESH)
    pl.semaphore_wait(barrier, len(peers))

    base_rows = pl.multiple_of((y * 4 + x) * 48, 16)
    ctl_rows = pl.multiple_of(y * 192, 16)
    arrays = ((bk, ck, K, TXH), (bq, cq, Q, 0), (bv, cv, V, TXH))
    for h in range(NH):
        for a, (bsrc, csrc, dst, off) in enumerate(arrays):
            for i in range(8):
                s = lax.rem(seq + i, 8)
                src = bsrc.at[0, :, pl.ds(pl.multiple_of(s * 384 + h * HD, HD), HD)]
                to = dst.at[h, pl.ds(off + base_rows, 48)]
                cp = remote(src, to, s1_base.at[a, h], s1_recv.at[a, h], {"grp": z, "seq": s, "rep": c})
                if i:
                    cp.start()
                else:
                    pl.when(yh == 1)(cp.start)
                    pl.when(yh == 0)(pltpu.make_async_copy(src, to, s1_recv.at[a, h]).start)
            for i in range(2):
                b = lax.rem(yl + i, 2)
                src = csrc.at[:, pl.ds(pl.multiple_of(b * 384 + h * HD, HD), HD)]
                to = dst.at[h, pl.ds(off + ctl_rows, 192)]
                cp = remote(src, to, s1_ctl.at[a, h], s1_recv.at[a, h], {"grp": z, "seq": b * 4 + x, "rep": 2 + c})
                if i:
                    cp.start()
                else:
                    pl.when(yh == 0)(cp.start)
                    pl.when(yh == 1)(pltpu.make_async_copy(src, to, s1_recv.at[a, h]).start)
    for cp in w_loc:
        cp.start()

    kv = ((0, K), (2, V))

    def exchange(i, h, k):
        buf = kv[i][1]
        lo = TXH + (0, 0, 2 * OWN)[k]
        to = TXH + (OWN, 2 * OWN, 3 * OWN)[k]
        return remote(
            buf.at[h, pl.ds(lo, OWN)], buf.at[h, pl.ds(to, OWN)],
            ex_send.at[i, h, k], ex_recv.at[i, h, k], (sib, dev_a, sib)[k],
        )

    def exchange_q(h):
        return remote(Q.at[h, pl.ds(0, OWN)], Q.at[h, pl.ds(OWN, OWN)], q_send.at[h], q_recv.at[h], dev_b)

    def pass_on(h):
        wait_bytes(K.at[h, pl.ds(TXH, OWN)], s1_recv.at[0, h])
        exchange(0, h, 1).start()
        exchange(0, h, 0).start()
        wait_bytes(Q.at[h, pl.ds(0, OWN)], s1_recv.at[1, h])
        exchange_q(h).start()
        wait_bytes(V.at[h, pl.ds(TXH, OWN)], s1_recv.at[2, h])
        exchange(1, h, 1).start()
        exchange(1, h, 0).start()

    def pass_second(h):
        for i in range(2):
            exchange(i, h, 1).wait_recv()
            exchange(i, h, 2).start()

    text_ok = lax.broadcasted_iota(jnp.int32, (ROWS, TXH), 1) + thalf * TXH < tl[0]

    def scores(h, r, lo, n):
        s = lax.dot_general(
            Q[h, pl.ds(r, ROWS)], K[h, pl.ds(lo, n)], NT, preferred_element_type=jnp.float32
        )
        if lo == 0:
            s = jnp.concatenate([jnp.where(text_ok, s[:, :TXH], -1e30), s[:, TXH:]], axis=1)
        return s

    def fold(h, r, s, lo, n):
        rows = pl.ds(r, ROWS)
        top = jnp.broadcast_to(jnp.max(s, axis=1, keepdims=True), (ROWS, HD))
        if lo:
            old = M[h, rows]
            top = jnp.maximum(old, top)
            f = jnp.exp2((old - top) * C2)
        M[h, rows] = top
        w = jnp.exp2((s - top[:, :1]) * C2)
        part = w[:, :HD]
        for i in range(1, n // HD):
            part = part + w[:, i * HD:(i + 1) * HD]
        got = jnp.dot(w.astype(jnp.bfloat16), V[h, pl.ds(lo, n)], preferred_element_type=jnp.float32)
        if lo:
            L[h, rows] = L[h, rows] * f + part
            A[h, rows] = A[h, rows] * f + got
        else:
            L[h, rows] = part
            A[h, rows] = got

    def tiles(h, starts, lo, n):
        s = scores(h, starts[0], lo, n)
        for i, r in enumerate(starts):
            later = scores(h, starts[i + 1], lo, n) if i + 1 < len(starts) else None
            fold(h, r, s, lo, n)
            s = later

    def send_part(h):
        return [
            remote(PO.at[h], RO.at[h], p_send.at[0, h], p_recv.at[0, h], dev_b),
            remote(PS.at[h], RS.at[h], p_send.at[1, h], p_recv.at[1, h], dev_b),
        ]

    def phase_a(h):
        for i in range(2):
            exchange(i, h, 0).wait_recv()
            wait_bytes((K, V)[i].at[h, pl.ds(0, TXH)], loc.at[3 + i * NH + h])
        exchange_q(h).wait_recv()
        tiles(h, (0, 384, 768, 1152), 0, KA)

    def phase_b(h):
        for i in range(2):
            exchange(i, h, 2).wait_recv()
        tiles(h, (768, 1152, 0, 384), KA, 2 * OWN)
        for i in range(OWN // HD):
            rows = pl.ds(OWN + i * HD, HD)
            total = jnp.broadcast_to(jnp.sum(L[h, rows], axis=1, keepdims=True), (HD, HD))
            PO[h, pl.ds(i * HD, HD)] = (A[h, rows] / total).astype(jnp.bfloat16)
            PS[h, pl.ds(i, 1)] = (M[h, rows] * C2 + jnp.log2(total)).T[:1]
        for i in range(OWN // HD, 8):
            PS[h, pl.ds(i, 1)] = jnp.zeros((1, HD), jnp.float32)
        for cp in send_part(h):
            cp.start()

    def give(h, i):
        to = lax.rem(y + i, 4)
        src = O.at[h, pl.ds(pl.multiple_of(to * 192, 16), 192)]
        dst = OG.at[yh, :, pl.ds(pl.multiple_of(yl * 384 + h * HD, HD), HD)]
        if i == 0:
            return pltpu.make_async_copy(src, dst, g_recv.at[yh])
        return remote(src, dst, g_send.at[h, i], g_recv.at[yh], dev(x, to, z, c))

    def merge(h):
        for cp in send_part(h):
            cp.wait_recv()
        for i in range(OWN // HD):
            rows = pl.ds(i * HD, HD)
            total = jnp.broadcast_to(jnp.sum(L[h, rows], axis=1, keepdims=True), (HD, HD))
            mine = M[h, rows] * C2 + jnp.log2(total)
            theirs = jnp.broadcast_to(RS[h, pl.ds(i, 1)], (HD, HD)).T
            top = jnp.maximum(mine, theirs)
            u, v = jnp.exp2(mine - top), jnp.exp2(theirs - top)
            value = A[h, rows] * (u / total) + RO[h, rows].astype(jnp.float32) * v
            O[h, rows] = (value / (u + v)).astype(jnp.bfloat16)
        for i in range(4):
            give(h, i).start()

    w_half = pl.ds(pl.multiple_of(c * 192, 16), 192)
    w_cp = remote(
        wb.at[w_half], WX.at[pl.ds(pl.multiple_of(yl * 384 + c * 192, 16), 192)],
        w_send.at[0], w_recv.at[0], dev(x, lax.rem(y + 3 + 2 * c, 4), z, c),
    )
    w_got = WX.at[pl.ds(pl.multiple_of((1 - yl) * 384 + c * 192, 16), 192)]
    w_sib = WX.at[pl.ds(pl.multiple_of((1 - yl) * 384 + (1 - c) * 192, 16), 192)]
    w_fwd = remote(w_got, w_got, w_send.at[1], w_recv.at[1], sib)

    pass_on(0)
    phase_a(0)
    pass_on(1)
    phase_a(1)
    pass_second(0)
    pass_on(2)
    w_cp.start()
    phase_b(0)
    phase_a(2)
    pass_second(1)
    merge(0)
    phase_b(1)
    pass_second(2)
    merge(1)
    phase_b(2)
    wait_bytes(w_got, w_recv.at[0])
    w_fwd.start()
    merge(2)

    def scatter(k, n, i):
        cols = pl.ds(n * CH, CH)
        if k == 0:
            to = lax.rem(x + i, 4)
            return remote(
                SB.at[pl.ds(pl.multiple_of(to * 48, 16), 48), cols], RB.at[i - 1, :, cols],
                r_send.at[k, n, i - 1], r_recv.at[k, n], dev(to, y, z, c),
            )
        to = lax.rem(z + i, 4)
        return remote(
            SC.at[pl.ds(pl.multiple_of(to * 48, 16), 48), cols], RC.at[i - 1, :, cols],
            r_send.at[k, n, i - 1], r_recv.at[k, n], dev(x, y, to, c),
        )

    for cp in w_loc:
        cp.wait()
    wait_bytes(w_sib, w_recv.at[1])
    wait_bytes(OG.at[0], g_recv.at[0])
    wait_bytes(OG.at[1], g_recv.at[1])
    for n in range(3072 // CH):
        cols = pl.ds(n * CH, CH)
        got = jnp.dot(OG[0], WX[:, cols], preferred_element_type=jnp.float32)
        SB[:, cols] = (gates[0:1, cols] * got).astype(jnp.bfloat16)
        for i in range(1, 4):
            scatter(0, n, i).start()
        got = gates[1:2, cols] * jnp.dot(OG[1], WC[:, cols], preferred_element_type=jnp.float32)
        got = got + jnp.where(z == n, HID[...].astype(jnp.float32), 0.0)
        SC[:, cols] = (gain[0:1, cols] * got).astype(jnp.bfloat16)
        for i in range(1, 4):
            scatter(1, n, i).start()
    for n in range(3072 // CH):
        cols = pl.ds(n * CH, CH)
        wait_bytes(RB.at[:, :, cols], r_recv.at[0, n])
        wait_bytes(RC.at[:, :, cols], r_recv.at[1, n])
        total = bh[0, :, cols].astype(jnp.float32)
        total = total + SB[pl.ds(pl.multiple_of(x * 48, 16), 48), cols].astype(jnp.float32)
        total = total + SC[pl.ds(pl.multiple_of(z * 48, 16), 48), cols].astype(jnp.float32)
        for i in range(3):
            total = total + RB[i, :, cols].astype(jnp.float32) + RC[i, :, cols].astype(jnp.float32)
        out[:, cols] = total.astype(jnp.bfloat16)

    for h in range(NH):
        for a in range(3):
            @pl.when(yh == 0)
            def _():
                wait_bytes(K.at[h, pl.ds(0, 7 * 48)], s1_base.at[a, h])
                wait_bytes(K.at[h, pl.ds(0, 384)], s1_ctl.at[a, h])

            @pl.when(yh == 1)
            def _():
                wait_bytes(K.at[h, pl.ds(0, 8 * 48)], s1_base.at[a, h])
                wait_bytes(K.at[h, pl.ds(0, 192)], s1_ctl.at[a, h])
        for i in range(2):
            for k in range(3):
                exchange(i, h, k).wait_send()
        exchange_q(h).wait_send()
        for cp in send_part(h):
            cp.wait_send()
        for i in range(1, 4):
            give(h, i).wait_send()
    w_cp.wait_send()
    w_fwd.wait_send()
    for n in range(3072 // CH):
        for k in range(2):
            for i in range(1, 4):
                scatter(k, n, i).wait_send()


def per_device(
    base_hidden, base_query, base_key, base_value, base_text_key, base_text_value, base_out_weight,
    control_hidden, control_query, control_key, control_value, control_text_key, control_text_value,
    control_out_weight, gate_table, control_gain, timestep, text_length,
):
    gates = lax.dynamic_index_in_dim(gate_table, timestep[0], 0, keepdims=False)
    bf, f32 = jnp.bfloat16, jnp.float32
    vm, hbm = pl.BlockSpec(memory_space=pltpu.VMEM), pl.BlockSpec(memory_space=pl.ANY)
    dma = pltpu.SemaphoreType.DMA
    out = pl.pallas_call(
        kernel,
        out_shape=jax.ShapeDtypeStruct((48, 3072), bf),
        in_specs=[pl.BlockSpec(memory_space=pltpu.SMEM), vm] + [hbm] * 13 + [vm, vm],
        out_specs=vm,
        scratch_shapes=[
            pltpu.VMEM((NH, 2 * OWN, HD), bf),
            pltpu.VMEM((NH, KALL, HD), bf),
            pltpu.VMEM((NH, KALL, HD), bf),
            pltpu.VMEM((NH, 2 * OWN, HD), f32),
            pltpu.VMEM((NH, 2 * OWN, HD), f32),
            pltpu.VMEM((NH, 2 * OWN, HD), f32),
            pltpu.VMEM((NH, OWN, HD), bf),
            pltpu.VMEM((NH, 8, HD), f32),
            pltpu.VMEM((NH, OWN, HD), bf),
            pltpu.VMEM((NH, 8, HD), f32),
            pltpu.VMEM((NH, OWN, HD), bf),
            pltpu.VMEM((2, 192, 768), bf),
            pltpu.VMEM((768, 3072), bf),
            pltpu.VMEM((768, 3072), bf),
            pltpu.VMEM((192, 768), bf),
            pltpu.VMEM((192, 3072), bf),
            pltpu.VMEM((192, 3072), bf),
            pltpu.VMEM((3, 48, 3072), bf),
            pltpu.VMEM((3, 48, 3072), bf),
            dma((3, NH)), dma((3, NH)), dma((3, NH)),
            dma((2, NH, 3)), dma((2, NH, 3)), dma((NH,)), dma((NH,)),
            dma((2, NH)), dma((2, NH)), dma((NH, 4)), dma((2,)),
            dma((2,)), dma((2,)), dma((2, 4, 3)), dma((2, 4)), dma((9,)),
        ],
        compiler_params=pltpu.CompilerParams(
            collective_id=0, has_side_effects=True, vmem_limit_bytes=56 * 2**20
        ),
        cost_estimate=pl.CostEstimate(flops=10**10, bytes_accessed=3 * 10**7, transcendentals=16 * 10**6),
    )(
        text_length, base_hidden, base_query, base_key, base_value, base_text_key, base_text_value,
        base_out_weight, control_hidden, control_query, control_key, control_value, control_text_key,
        control_text_value, control_out_weight, gates, control_gain.reshape(1, -1),
    )
    return out.reshape(1, 48, 3072)


def solution(mesh):
    rows, cols = P(("seq", "rep"), "grp", None), P(("seq", "rep"), "grp")
    placed = (
        rows, rows, rows, rows, P(None, "seq"), P(None, "seq"), P("seq", None),
        cols, cols, cols, cols, P(None, "grp"), P(None, "grp"), P("grp", None),
        P(), P(), P(), P(),
    )
    return jax.shard_map(per_device, mesh=mesh, in_specs=placed, out_specs=rows, check_vma=False)
```

```python
import math

import jax
import jax.numpy as jnp
from jax import lax
from jax.experimental import pallas as pl
from jax.experimental.pallas import tpu as pltpu
from jax.sharding import PartitionSpec as P

HD = 128
NH = 3
OWN = 768
TXH = 256
KA = TXH + 2 * OWN
KALL = TXH + 4 * OWN
ROWS = 384
PARTS = ((0, 16), (16, 32))
CH = 768
C2 = math.log2(math.e) / math.sqrt(HD)
NT = (((1,), (1,)), ((), ()))
MESH = pl.DeviceIdType.MESH


def remote(src, dst, ssem, rsem, dev):
    return pltpu.make_async_remote_copy(
        src_ref=src, dst_ref=dst, send_sem=ssem, recv_sem=rsem, device_id=dev, device_id_type=MESH
    )


def wait_bytes(ref, sem):
    pltpu.make_async_copy(ref, ref, sem).wait()


def kernel(
    tl, ts, bh, bq, bk, bv, btk, btv, wb, ch, cq, ck, cv, ctk, ctv, wc, table, gain, out,
    Q, K, V, M, L, A, PO, PS, RO, RS, O, OG0, OG1, WX, WC, HID, GT, SB0, SB1, SC0, SC1, RB0, RB1, RC0, RC1,
    s1_recv, s1_base, s1_ctl, ex_send, ex_recv, q_send, q_recv, p_send, p_recv,
    g_send, g_recv, w_send, w_recv, r_send, r_recv, loc,
):
    z = lax.axis_index("grp")
    seq = lax.axis_index("seq")
    rep = lax.axis_index("rep")
    x, yl = lax.rem(seq, 4), seq // 4
    yh, c = rep // 2, lax.rem(rep, 2)
    y = yh * 2 + yl

    def dev(xx, yy, zz, cc):
        return {"grp": zz, "seq": lax.rem(yy, 2) * 4 + xx, "rep": (yy // 2) * 2 + cc}

    sib = dev(x, y, z, 1 - c)
    pos = (1 - yh) * z + yh * x
    pa = pos + 1 - 2 * lax.rem(pos, 2)
    pb = lax.rem(pos + 3 - 2 * lax.rem(pos, 2), 4)
    dev_a = dev(yh * pa + (1 - yh) * x, y, (1 - yh) * pa + yh * z, c)
    dev_b = dev(yh * pb + (1 - yh) * x, y, (1 - yh) * pb + yh * z, c)
    thalf = pos // 2

    w_loc = [
        pltpu.make_async_copy(wc, WC, loc.at[0]),
        pltpu.make_async_copy(wb, WX.at[pl.ds(pl.multiple_of(yl * 384, 128), 384)], loc.at[1]),
        pltpu.make_async_copy(ch, HID, loc.at[2]),
        pltpu.make_async_copy(table, GT, loc.at[9]),
    ]

    def text_copies(h, is_base):
        rows = pl.ds(pl.multiple_of(thalf * TXH, TXH), TXH)
        if is_base:
            cols = pl.ds(h * HD, HD)
            srcs = (btk, btv)
        else:
            cols = pl.ds(pl.multiple_of(yl * 384 + h * HD, HD), HD)
            srcs = (ctk, ctv)
        return [
            pltpu.make_async_copy(srcs[i].at[rows, cols], (K, V)[i].at[h, pl.ds(0, TXH)], loc.at[3 + i * NH + h])
            for i in range(2)
        ]

    @pl.when(yh == 0)
    def _():
        for h in range(NH):
            for cp in text_copies(h, True):
                cp.start()

    @pl.when(yh == 1)
    def _():
        for h in range(NH):
            for cp in text_copies(h, False):
                cp.start()

    barrier = pltpu.get_barrier_semaphore()
    peers = [dev(lax.rem(x + i % 4, 4), lax.rem(y + i // 4, 4), z, c) for i in range(1, 16)]
    peers += [dev(x, y, lax.rem(z + i, 4), c) for i in range(1, 4)] + [sib]
    for d in peers:
        pl.semaphore_signal(barrier, inc=1, device_id=d, device_id_type=MESH)
    pl.semaphore_wait(barrier, len(peers))

    base_rows = pl.multiple_of((y * 4 + x) * 48, 16)
    ctl_rows = pl.multiple_of(y * 192, 16)
    arrays = ((bk, ck, K, TXH), (bq, cq, Q, 0), (bv, cv, V, TXH))
    def part_rows(p, block):
        first, count = PARTS[p]
        return pl.ds(pl.multiple_of(first * 16 + block * count, 16), count)

    def stage1(h):
        for a, (bsrc, csrc, dst, off) in enumerate(arrays):
            sem = s1_recv.at[a, h]
            for i in range(2):
                b = lax.rem(yl + i, 2)
                cols = pl.ds(pl.multiple_of(b * 384 + h * HD, HD), HD)
                if a == 1:
                    pieces = [
                        (csrc.at[pl.ds(q * 48 + PARTS[p][0], PARTS[p][1]), cols], dst.at[h, part_rows(p, y * 4 + q)])
                        for q in range(4) for p in range(2)
                    ]
                else:
                    pieces = [(csrc.at[:, cols], dst.at[h, pl.ds(off + ctl_rows, 192)])]
                for src, to in pieces:
                    cp = remote(src, to, s1_ctl.at[a, h], sem, {"grp": z, "seq": b * 4 + x, "rep": 2 + c})
                    if i:
                        cp.start()
                    else:
                        pl.when(yh == 0)(cp.start)
                        pl.when(yh == 1)(pltpu.make_async_copy(src, to, sem).start)
            for i in range(8):
                s = lax.rem(seq + i, 8)
                cols = pl.ds(pl.multiple_of(s * 384 + h * HD, HD), HD)
                if a == 1:
                    pieces = [
                        (bsrc.at[0, pl.ds(*PARTS[p]), cols], dst.at[h, part_rows(p, y * 4 + x)]) for p in range(2)
                    ]
                else:
                    pieces = [(bsrc.at[0, :, cols], dst.at[h, pl.ds(off + base_rows, 48)])]
                for src, to in pieces:
                    cp = remote(src, to, s1_base.at[a, h], sem, {"grp": z, "seq": s, "rep": c})
                    if i:
                        cp.start()
                    else:
                        pl.when(yh == 1)(cp.start)
                        pl.when(yh == 0)(pltpu.make_async_copy(src, to, sem).start)

    stage1(0)
    for cp in w_loc:
        cp.start()

    kv = ((0, K), (2, V))

    def exchange(i, h, k):
        buf = kv[i][1]
        lo = TXH + (0, 0, 2 * OWN)[k]
        to = TXH + (OWN, 2 * OWN, 3 * OWN)[k]
        return remote(
            buf.at[h, pl.ds(lo, OWN)], buf.at[h, pl.ds(to, OWN)],
            ex_send.at[i, h, k], ex_recv.at[i, h, k], (sib, dev_a, sib)[k],
        )

    def exchange_q(h):
        return remote(Q.at[h, pl.ds(0, OWN)], Q.at[h, pl.ds(OWN, OWN)], q_send.at[h], q_recv.at[h], dev_b)

    def pass_on(h):
        wait_bytes(K.at[h, pl.ds(TXH, OWN)], s1_recv.at[0, h])
        exchange(0, h, 1).start()
        exchange(0, h, 0).start()
        if h + 1 < NH:
            stage1(h + 1)
        wait_bytes(Q.at[h, pl.ds(0, OWN)], s1_recv.at[1, h])
        exchange_q(h).start()
        wait_bytes(V.at[h, pl.ds(TXH, OWN)], s1_recv.at[2, h])
        exchange(1, h, 1).start()
        exchange(1, h, 0).start()

    def pass_second(h):
        for i in range(2):
            exchange(i, h, 1).wait_recv()
            exchange(i, h, 2).start()

    text_ok = lax.broadcasted_iota(jnp.int32, (ROWS, TXH), 1) + thalf * TXH < tl[0]

    def scores(h, r, size, lo, n):
        s = lax.dot_general(
            Q[h, pl.ds(r, size)], K[h, pl.ds(lo, n)], NT, preferred_element_type=jnp.float32
        )
        if lo == 0:
            s = jnp.concatenate([jnp.where(text_ok, s[:, :TXH], -1e30), s[:, TXH:]], axis=1)
        return s

    def fold(h, r, size, s, lo, n):
        rows = pl.ds(r, size)
        top = jnp.broadcast_to(jnp.max(s, axis=1, keepdims=True), (size, HD))
        if lo:
            old = M[h, rows]
            top = jnp.maximum(old, top)
            f = jnp.exp2((old - top) * C2)
        M[h, rows] = top
        w = jnp.exp2((s - top[:, :1]) * C2)
        part = w[:, :HD]
        for i in range(1, n // HD):
            part = part + w[:, i * HD:(i + 1) * HD]
        got = jnp.dot(w.astype(jnp.bfloat16), V[h, pl.ds(lo, n)], preferred_element_type=jnp.float32)
        if lo:
            L[h, rows] = L[h, rows] * f + part
            A[h, rows] = A[h, rows] * f + got
        else:
            L[h, rows] = part
            A[h, rows] = got

    def tiles(h, todo, lo, n):
        s = scores(h, *todo[0][:2], lo, n)
        for i, (r, size, then) in enumerate(todo):
            later = scores(h, *todo[i + 1][:2], lo, n) if i + 1 < len(todo) else None
            fold(h, r, size, s, lo, n)
            if then is not None:
                then()
            s = later

    def part_span(p):
        return PARTS[p][0] * 16, PARTS[p][1] * 16

    def send_part(h, p):
        rows = pl.ds(*part_span(p))
        return [
            remote(PO.at[h, rows], RO.at[h, rows], p_send.at[0, h, p], p_recv.at[0, h, p], dev_b),
            remote(PS.at[h, p], RS.at[h, p], p_send.at[1, h, p], p_recv.at[1, h, p], dev_b),
        ]

    def log_sum(h, rows):
        total = jnp.broadcast_to(jnp.sum(L[h, rows], axis=1, keepdims=True), (HD, HD))
        return total, M[h, rows] * C2 + jnp.log2(total)

    def hand_over(h, p):
        first, count = part_span(p)
        for i in range(count // HD):
            rows = pl.ds(OWN + first + i * HD, HD)
            total, both = log_sum(h, rows)
            PO[h, pl.ds(first + i * HD, HD)] = (A[h, rows] / total).astype(jnp.bfloat16)
            PS[h, p, pl.ds(i, 1)] = both.T[:1]
        for i in range(count // HD, 8):
            PS[h, p, pl.ds(i, 1)] = jnp.zeros((1, HD), jnp.float32)
        for cp in send_part(h, p):
            cp.start()

    def phase_a(h):
        for i in range(2):
            exchange(i, h, 0).wait_recv()
            wait_bytes((K, V)[i].at[h, pl.ds(0, TXH)], loc.at[3 + i * NH + h])
        near, far = [(0, ROWS, None), (ROWS, ROWS, None)], [(OWN, ROWS, None), (OWN + ROWS, ROWS, None)]
        if h == 0:
            tiles(h, near, 0, KA)
            exchange_q(h).wait_recv()
            tiles(h, far, 0, KA)
        else:
            exchange_q(h).wait_recv()
            tiles(h, near + far, 0, KA)

    def phase_b(h):
        for i in range(2):
            exchange(i, h, 2).wait_recv()

        def over():
            for p in range(2):
                hand_over(h, p)

        if h + 1 < NH:
            todo = [(OWN, ROWS, None), (OWN + ROWS, ROWS, over), (0, ROWS, None), (ROWS, ROWS, None)]
        else:
            todo = [(OWN + part_span(p)[0], part_span(p)[1], lambda p=p: hand_over(h, p)) for p in range(2)]
            todo += [(*part_span(p), None) for p in range(2)]
        tiles(h, todo, KA, 2 * OWN)

    OG = (OG0, OG1)

    def give(h, p, i):
        to = lax.rem(y + i, 4)
        first, count = PARTS[p]
        src = O.at[h, pl.ds(pl.multiple_of(first * 16 + to * 4 * count, 16), 4 * count)]
        dst = OG[p].at[yh, :, pl.ds(pl.multiple_of(yl * 384 + h * HD, HD), HD)]
        if i == 0:
            return pltpu.make_async_copy(src, dst, g_recv.at[p, yh])
        return remote(src, dst, g_send.at[h, p, i], g_recv.at[p, yh], dev(x, to, z, c))

    def merge(h, p):
        for cp in send_part(h, p):
            cp.wait_recv()
        first, count = part_span(p)
        for i in range(count // HD):
            rows = pl.ds(first + i * HD, HD)
            total, mine = log_sum(h, rows)
            theirs = jnp.broadcast_to(RS[h, p, pl.ds(i, 1)], (HD, HD)).T
            top = jnp.maximum(mine, theirs)
            u, v = jnp.exp2(mine - top), jnp.exp2(theirs - top)
            value = A[h, rows] * (u / total) + RO[h, rows].astype(jnp.float32) * v
            O[h, rows] = (value / (u + v)).astype(jnp.bfloat16)
        for i in range(4):
            give(h, p, i).start()

    w_half = pl.ds(pl.multiple_of(c * 192, 16), 192)
    w_cp = remote(
        wb.at[w_half], WX.at[pl.ds(pl.multiple_of(yl * 384 + c * 192, 16), 192)],
        w_send.at[0], w_recv.at[0], dev(x, lax.rem(y + 3 + 2 * c, 4), z, c),
    )
    w_got = WX.at[pl.ds(pl.multiple_of((1 - yl) * 384 + c * 192, 16), 192)]
    w_sib = WX.at[pl.ds(pl.multiple_of((1 - yl) * 384 + (1 - c) * 192, 16), 192)]
    w_fwd = remote(w_got, w_got, w_send.at[1], w_recv.at[1], sib)

    pass_on(0)
    phase_a(0)
    pass_on(1)
    pass_second(0)
    phase_b(0)
    pass_on(2)
    w_cp.start()
    phase_a(1)
    pass_second(1)
    phase_b(1)
    merge(0, 0)
    merge(0, 1)
    phase_a(2)
    pass_second(2)
    wait_bytes(w_got, w_recv.at[0])
    w_fwd.start()
    merge(1, 0)
    merge(1, 1)
    phase_b(2)
    merge(2, 0)
    merge(2, 1)

    S = ((SB0, SC0), (SB1, SC1))
    R = ((RB0, RC0), (RB1, RC1))

    def scatter(p, k, n, i):
        cols = pl.ds(n * CH, CH)
        count = PARTS[p][1]
        to = lax.rem((x, z)[k] + i, 4)
        return remote(
            S[p][k].at[pl.ds(pl.multiple_of(to * count, 16), count), cols], R[p][k].at[i - 1, :, cols],
            r_send.at[p, k, n, i - 1], r_recv.at[p, k, n], dev(to, y, z, c) if k == 0 else dev(x, y, to, c),
        )

    for cp in w_loc:
        cp.wait()
    wait_bytes(w_sib, w_recv.at[1])
    step = ts[0]
    for p in range(2):
        first, count = PARTS[p]
        wait_bytes(OG[p].at[0], g_recv.at[p, 0])
        wait_bytes(OG[p].at[1], g_recv.at[p, 1])
        hidden = jnp.concatenate([HID[pl.ds(q * 48 + first, count)] for q in range(4)], axis=0).astype(jnp.float32)
        for n in range(3072 // CH):
            cols = pl.ds(n * CH, CH)
            got = jnp.dot(OG[p][0], WX[:, cols], preferred_element_type=jnp.float32)
            S[p][0][:, cols] = (GT[step, 0:1, cols] * got).astype(jnp.bfloat16)
            for i in range(1, 4):
                scatter(p, 0, n, i).start()
            got = GT[step, 1:2, cols] * jnp.dot(OG[p][1], WC[:, cols], preferred_element_type=jnp.float32)
            got = got + jnp.where(z == n, hidden, 0.0)
            S[p][1][:, cols] = (gain[0:1, cols] * got).astype(jnp.bfloat16)
            for i in range(1, 4):
                scatter(p, 1, n, i).start()
    for p in range(2):
        first, count = PARTS[p]
        for n in range(3072 // CH):
            cols = pl.ds(n * CH, CH)
            total = bh[0, pl.ds(first, count), cols].astype(jnp.float32)
            for k in range(2):
                wait_bytes(R[p][k].at[:, :, cols], r_recv.at[p, k, n])
                own = pl.ds(pl.multiple_of((x, z)[k] * count, 16), count)
                total = total + S[p][k][own, cols].astype(jnp.float32)
                for i in range(3):
                    total = total + R[p][k][i, :, cols].astype(jnp.float32)
            out[pl.ds(first, count), cols] = total.astype(jnp.bfloat16)

    for h in range(NH):
        for a in range(3):
            @pl.when(yh == 0)
            def _():
                wait_bytes(K.at[h, pl.ds(0, 7 * 48)], s1_base.at[a, h])
                wait_bytes(K.at[h, pl.ds(0, 384)], s1_ctl.at[a, h])

            @pl.when(yh == 1)
            def _():
                wait_bytes(K.at[h, pl.ds(0, 8 * 48)], s1_base.at[a, h])
                wait_bytes(K.at[h, pl.ds(0, 192)], s1_ctl.at[a, h])
        for i in range(2):
            for k in range(3):
                exchange(i, h, k).wait_send()
        exchange_q(h).wait_send()
        for p in range(2):
            for cp in send_part(h, p):
                cp.wait_send()
            for i in range(1, 4):
                give(h, p, i).wait_send()
    w_cp.wait_send()
    w_fwd.wait_send()
    for n in range(3072 // CH):
        for p in range(2):
            for k in range(2):
                for i in range(1, 4):
                    scatter(p, k, n, i).wait_send()


def per_device(
    base_hidden, base_query, base_key, base_value, base_text_key, base_text_value, base_out_weight,
    control_hidden, control_query, control_key, control_value, control_text_key, control_text_value,
    control_out_weight, gate_table, control_gain, timestep, text_length,
):
    bf, f32 = jnp.bfloat16, jnp.float32
    vm, hbm = pl.BlockSpec(memory_space=pltpu.VMEM), pl.BlockSpec(memory_space=pl.ANY)
    dma = pltpu.SemaphoreType.DMA
    out = pl.pallas_call(
        kernel,
        out_shape=jax.ShapeDtypeStruct((48, 3072), bf),
        in_specs=[pl.BlockSpec(memory_space=pltpu.SMEM)] * 2 + [vm] + [hbm] * 14 + [vm],
        out_specs=vm,
        scratch_shapes=[
            pltpu.VMEM((NH, 2 * OWN, HD), bf),
            pltpu.VMEM((NH, KALL, HD), bf),
            pltpu.VMEM((NH, KALL, HD), bf),
            pltpu.VMEM((NH, 2 * OWN, HD), f32),
            pltpu.VMEM((NH, 2 * OWN, HD), f32),
            pltpu.VMEM((NH, 2 * OWN, HD), f32),
            pltpu.VMEM((NH, OWN, HD), bf),
            pltpu.VMEM((NH, 2, 8, HD), f32),
            pltpu.VMEM((NH, OWN, HD), bf),
            pltpu.VMEM((NH, 2, 8, HD), f32),
            pltpu.VMEM((NH, OWN, HD), bf),
            pltpu.VMEM((2, 64, 768), bf),
            pltpu.VMEM((2, 128, 768), bf),
            pltpu.VMEM((768, 3072), bf),
            pltpu.VMEM((768, 3072), bf),
            pltpu.VMEM((192, 768), bf),
            pltpu.VMEM((28, 2, 3072), f32),
            pltpu.VMEM((64, 3072), bf),
            pltpu.VMEM((128, 3072), bf),
            pltpu.VMEM((64, 3072), bf),
            pltpu.VMEM((128, 3072), bf),
            pltpu.VMEM((3, 16, 3072), bf),
            pltpu.VMEM((3, 32, 3072), bf),
            pltpu.VMEM((3, 16, 3072), bf),
            pltpu.VMEM((3, 32, 3072), bf),
            dma((3, NH)), dma((3, NH)), dma((3, NH)),
            dma((2, NH, 3)), dma((2, NH, 3)), dma((NH,)), dma((NH,)),
            dma((2, NH, 2)), dma((2, NH, 2)), dma((NH, 2, 4)), dma((2, 2)),
            dma((2,)), dma((2,)), dma((2, 2, 4, 3)), dma((2, 2, 4)), dma((10,)),
        ],
        compiler_params=pltpu.CompilerParams(
            collective_id=0, has_side_effects=True, vmem_limit_bytes=56 * 2**20
        ),
        cost_estimate=pl.CostEstimate(flops=10**10, bytes_accessed=3 * 10**7, transcendentals=16 * 10**6),
    )(
        text_length, timestep, base_hidden, base_query, base_key, base_value, base_text_key, base_text_value,
        base_out_weight, control_hidden, control_query, control_key, control_value, control_text_key,
        control_text_value, control_out_weight, gate_table, control_gain.reshape(1, -1),
    )
    return out.reshape(1, 48, 3072)


def solution(mesh):
    rows, cols = P(("seq", "rep"), "grp", None), P(("seq", "rep"), "grp")
    placed = (
        rows, rows, rows, rows, P(None, "seq"), P(None, "seq"), P("seq", None),
        cols, cols, cols, cols, P(None, "grp"), P(None, "grp"), P("grp", None),
        P(), P(), P(), P(),
    )
    return jax.shard_map(per_device, mesh=mesh, in_specs=placed, out_specs=rows, check_vma=False)
```

```python
import math

import jax
import jax.numpy as jnp
from jax import lax
from jax.experimental import pallas as pl
from jax.experimental.pallas import tpu as pltpu
from jax.sharding import PartitionSpec as P

HD = 128
NH = 3
OWN = 768
TXH = 256
KA = TXH + 2 * OWN
KALL = TXH + 4 * OWN
ROWS = 384
PARTS = ((0, 16), (16, 32))
CH = 768
C2 = math.log2(math.e) / math.sqrt(HD)
BLOCK = ((0, KA), (KA, 2 * OWN))
NT = (((1,), (1,)), ((), ()))
MESH = pl.DeviceIdType.MESH


def remote(src, dst, ssem, rsem, dev):
    return pltpu.make_async_remote_copy(
        src_ref=src, dst_ref=dst, send_sem=ssem, recv_sem=rsem, device_id=dev, device_id_type=MESH
    )


def wait_bytes(ref, sem):
    pltpu.make_async_copy(ref, ref, sem).wait()


def kernel(
    tl, ts, bh, bq, bk, bv, btk, btv, wb, ch, cq, ck, cv, ctk, ctv, wc, table, gain, out,
    Q, K, V, M, L, A, PO, PS, RO, RS, O, OG0, OG1, WX, WC, HID, GT, SB0, SB1, SC0, SC1, RB0, RB1, RC0, RC1,
    s1_recv, s1_base, s1_ctl, ex_send, ex_recv, q_send, q_recv, p_send, p_recv,
    g_send, g_recv, w_send, w_recv, r_send, r_recv, loc,
):
    z = lax.axis_index("grp")
    seq = lax.axis_index("seq")
    rep = lax.axis_index("rep")
    x, yl = lax.rem(seq, 4), seq // 4
    yh, c = rep // 2, lax.rem(rep, 2)
    y = yh * 2 + yl

    def dev(xx, yy, zz, cc):
        return {"grp": zz, "seq": lax.rem(yy, 2) * 4 + xx, "rep": (yy // 2) * 2 + cc}

    sib = dev(x, y, z, 1 - c)
    pos = (1 - yh) * z + yh * x
    pa = pos + 1 - 2 * lax.rem(pos, 2)
    pb = lax.rem(pos + 3 - 2 * lax.rem(pos, 2), 4)
    dev_a = dev(yh * pa + (1 - yh) * x, y, (1 - yh) * pa + yh * z, c)
    dev_b = dev(yh * pb + (1 - yh) * x, y, (1 - yh) * pb + yh * z, c)
    kv_dev, q_dev = (dev_a, dev_a, dev_b), (dev_b, dev_b, dev_a)
    thalf = (pos // 2, pos // 2, lax.rem(pos + 1, 4) // 2)

    w_loc = [
        pltpu.make_async_copy(wc, WC, loc.at[0]),
        pltpu.make_async_copy(wb, WX.at[pl.ds(pl.multiple_of(yl * 384, 128), 384)], loc.at[1]),
        pltpu.make_async_copy(ch, HID, loc.at[2]),
        pltpu.make_async_copy(table, GT, loc.at[9]),
    ]

    def text_copies(h, is_base):
        rows = pl.ds(pl.multiple_of(thalf[h] * TXH, TXH), TXH)
        if is_base:
            cols = pl.ds(h * HD, HD)
            srcs = (btk, btv)
        else:
            cols = pl.ds(pl.multiple_of(yl * 384 + h * HD, HD), HD)
            srcs = (ctk, ctv)
        return [
            pltpu.make_async_copy(srcs[i].at[rows, cols], (K, V)[i].at[h, pl.ds(0, TXH)], loc.at[3 + i * NH + h])
            for i in range(2)
        ]

    @pl.when(yh == 0)
    def _():
        for h in range(NH):
            for cp in text_copies(h, True):
                cp.start()

    @pl.when(yh == 1)
    def _():
        for h in range(NH):
            for cp in text_copies(h, False):
                cp.start()

    barrier = pltpu.get_barrier_semaphore()
    peers = [dev(lax.rem(x + i % 4, 4), lax.rem(y + i // 4, 4), z, c) for i in range(1, 16)]
    peers += [dev(x, y, lax.rem(z + i, 4), c) for i in range(1, 4)] + [sib]
    for d in peers:
        pl.semaphore_signal(barrier, inc=1, device_id=d, device_id_type=MESH)
    pl.semaphore_wait(barrier, len(peers))

    base_rows = pl.multiple_of((y * 4 + x) * 48, 16)
    ctl_rows = pl.multiple_of(y * 192, 16)
    arrays = ((bk, ck, K, TXH), (bq, cq, Q, 0), (bv, cv, V, TXH))
    def part_rows(p, block):
        first, count = PARTS[p]
        return pl.ds(pl.multiple_of(first * 16 + block * count, 16), count)

    def stage1(h, a):
        bsrc, csrc, dst, off = arrays[a]
        sem = s1_recv.at[a, h]
        for i in range(2):
            b = lax.rem(yl + i, 2)
            cols = pl.ds(pl.multiple_of(b * 384 + h * HD, HD), HD)
            if a == 1:
                pieces = [
                    (csrc.at[pl.ds(q * 48 + PARTS[p][0], PARTS[p][1]), cols], dst.at[h, part_rows(p, y * 4 + q)])
                    for q in range(4) for p in range(2)
                ]
            else:
                pieces = [(csrc.at[:, cols], dst.at[h, pl.ds(off + ctl_rows, 192)])]
            for src, to in pieces:
                cp = remote(src, to, s1_ctl.at[a, h], sem, {"grp": z, "seq": b * 4 + x, "rep": 2 + c})
                if i:
                    cp.start()
                else:
                    pl.when(yh == 0)(cp.start)
                    pl.when(yh == 1)(pltpu.make_async_copy(src, to, sem).start)
        for i in range(8):
            s = lax.rem(seq + i, 8)
            cols = pl.ds(pl.multiple_of(s * 384 + h * HD, HD), HD)
            if a == 1:
                pieces = [
                    (bsrc.at[0, pl.ds(*PARTS[p]), cols], dst.at[h, part_rows(p, y * 4 + x)]) for p in range(2)
                ]
            else:
                pieces = [(bsrc.at[0, :, cols], dst.at[h, pl.ds(off + base_rows, 48)])]
            for src, to in pieces:
                cp = remote(src, to, s1_base.at[a, h], sem, {"grp": z, "seq": s, "rep": c})
                if i:
                    cp.start()
                else:
                    pl.when(yh == 1)(cp.start)
                    pl.when(yh == 0)(pltpu.make_async_copy(src, to, sem).start)

    for a in range(3):
        stage1(0, a)
    for cp in w_loc:
        cp.start()

    kv = ((0, K), (2, V))

    def exchange(i, h, k):
        buf = kv[i][1]
        lo = TXH + (0, 0, 2 * OWN)[k]
        to = TXH + (OWN, 2 * OWN, 3 * OWN)[k]
        return remote(
            buf.at[h, pl.ds(lo, OWN)], buf.at[h, pl.ds(to, OWN)],
            ex_send.at[i, h, k], ex_recv.at[i, h, k], (sib, kv_dev[h], sib)[k],
        )

    def exchange_q(h):
        return remote(Q.at[h, pl.ds(0, OWN)], Q.at[h, pl.ds(OWN, OWN)], q_send.at[h], q_recv.at[h], q_dev[h])

    def landed(h, a):
        dst, off = arrays[a][2:]
        wait_bytes(dst.at[h, pl.ds(off, OWN)], s1_recv.at[a, h])
        if a == 0 and h + 1 < NH:
            for i in range(3):
                stage1(h + 1, i)
        if a == 1:
            exchange_q(h).start()
        else:
            exchange(a // 2, h, 1).start()
            exchange(a // 2, h, 0).start()

    def second(h, i):
        exchange(i, h, 1).wait_recv()
        exchange(i, h, 2).start()

    text_at = lax.broadcasted_iota(jnp.int32, (ROWS, TXH), 1)

    def scores(h, r, size, lo, n):
        s = lax.dot_general(
            Q[h, pl.ds(r, size)], K[h, pl.ds(lo, n)], NT, preferred_element_type=jnp.float32
        )
        if lo == 0:
            s = jnp.concatenate([jnp.where(text_at + thalf[h] * TXH < tl[0], s[:, :TXH], -1e30), s[:, TXH:]], axis=1)
        return s

    def fold(h, r, size, s, lo, n):
        rows = pl.ds(r, size)
        top = jnp.broadcast_to(jnp.max(s, axis=1, keepdims=True), (size, HD))
        if lo:
            old = M[h, rows]
            top = jnp.maximum(old, top)
            f = jnp.exp2((old - top) * C2)
        M[h, rows] = top
        w = jnp.exp2((s - top[:, :1]) * C2)
        part = w[:, :HD]
        for i in range(1, n // HD):
            part = part + w[:, i * HD:(i + 1) * HD]
        got = jnp.dot(w.astype(jnp.bfloat16), V[h, pl.ds(lo, n)], preferred_element_type=jnp.float32)
        if lo:
            L[h, rows] = L[h, rows] * f + part
            A[h, rows] = A[h, rows] * f + got
        else:
            L[h, rows] = part
            A[h, rows] = got

    def tiles(todo):
        def first(item):
            h, b, r, size, before, _ = item
            if before is not None:
                before()
            return scores(h, r, size, *BLOCK[b])

        s = first(todo[0])
        for i, (h, b, r, size, _, after) in enumerate(todo):
            later = first(todo[i + 1]) if i + 1 < len(todo) else None
            fold(h, r, size, s, *BLOCK[b])
            if after is not None:
                after()
            s = later

    def part_span(p):
        return PARTS[p][0] * 16, PARTS[p][1] * 16

    def send_part(h, p):
        rows = pl.ds(*part_span(p))
        return [
            remote(PO.at[h, rows], RO.at[h, rows], p_send.at[0, h, p], p_recv.at[0, h, p], q_dev[h]),
            remote(PS.at[h, p], RS.at[h, p], p_send.at[1, h, p], p_recv.at[1, h, p], q_dev[h]),
        ]

    eye = lax.broadcasted_iota(jnp.int32, (HD, HD), 0) == lax.broadcasted_iota(jnp.int32, (HD, HD), 1)

    def log_sum(h, rows):
        total = jnp.broadcast_to(jnp.sum(L[h, rows], axis=1, keepdims=True), (HD, HD))
        return total, M[h, rows] * C2 + jnp.log2(total)

    def hand_over(h, p):
        first, count = part_span(p)
        for i in range(count // HD):
            rows = pl.ds(OWN + first + i * HD, HD)
            total, both = log_sum(h, rows)
            PO[h, pl.ds(first + i * HD, HD)] = (A[h, rows] / total).astype(jnp.bfloat16)
            PS[h, p, pl.ds(i, 1)] = jnp.sum(jnp.where(eye, both, 0.0), axis=0, keepdims=True)
        for i in range(count // HD, 8):
            PS[h, p, pl.ds(i, 1)] = jnp.zeros((1, HD), jnp.float32)
        for cp in send_part(h, p):
            cp.start()

    def have_near(h):
        for i in range(2):
            exchange(i, h, 0).wait_recv()
            wait_bytes((K, V)[i].at[h, pl.ds(0, TXH)], loc.at[3 + i * NH + h])

    def have_far(h):
        for i in range(2):
            exchange(i, h, 2).wait_recv()

    def unit(h, b, far, before=None, mid=None, after=None):
        r = far * OWN
        return [(h, b, r, ROWS, before, mid), (h, b, r + ROWS, ROWS, None, after)]

    def do(*steps):
        def run():
            for f, *args in steps:
                f(*args)
        return run

    OG = (OG0, OG1)

    def give(h, p, i):
        to = lax.rem(y + i, 4)
        first, count = PARTS[p]
        src = O.at[h, pl.ds(pl.multiple_of(first * 16 + to * 4 * count, 16), 4 * count)]
        dst = OG[p].at[yh, :, pl.ds(pl.multiple_of(yl * 384 + h * HD, HD), HD)]
        if i == 0:
            return pltpu.make_async_copy(src, dst, g_recv.at[p, yh])
        return remote(src, dst, g_send.at[h, p, i], g_recv.at[p, yh], dev(x, to, z, c))

    def merge(h, p):
        for cp in send_part(h, p):
            cp.wait_recv()
        first, count = part_span(p)
        for i in range(count // HD):
            rows = pl.ds(first + i * HD, HD)
            total, mine = log_sum(h, rows)
            theirs = jnp.sum(jnp.where(eye, RS[h, p, pl.ds(i, 1)], 0.0), axis=1, keepdims=True)
            theirs = jnp.broadcast_to(theirs, (HD, HD))
            top = jnp.maximum(mine, theirs)
            u, v = jnp.exp2(mine - top), jnp.exp2(theirs - top)
            value = A[h, rows] * (u / total) + RO[h, rows].astype(jnp.float32) * v
            O[h, rows] = (value / (u + v)).astype(jnp.bfloat16)
        for i in range(4):
            give(h, p, i).start()

    w_half = pl.ds(pl.multiple_of(c * 192, 16), 192)
    w_cp = remote(
        wb.at[w_half], WX.at[pl.ds(pl.multiple_of(yl * 384 + c * 192, 16), 192)],
        w_send.at[0], w_recv.at[0], dev(x, lax.rem(y + 3 + 2 * c, 4), z, c),
    )
    w_got = WX.at[pl.ds(pl.multiple_of((1 - yl) * 384 + c * 192, 16), 192)]
    w_sib = WX.at[pl.ds(pl.multiple_of((1 - yl) * 384 + (1 - c) * 192, 16), 192)]
    w_fwd = remote(w_got, w_got, w_send.at[1], w_recv.at[1], sib)

    landed(0, 0)
    landed(0, 1)
    landed(0, 2)
    have_near(0)
    tiles(unit(0, 0, 0, mid=do((landed, 1, 0)), after=do((second, 0, 0))))
    exchange_q(0).wait_recv()
    tiles(unit(0, 0, 1, mid=do((landed, 1, 1)), after=do((second, 0, 1), (landed, 1, 2))))
    have_far(0)
    tiles(
        unit(0, 1, 1, after=do((hand_over, 0, 0), (hand_over, 0, 1), (landed, 2, 0)))
        + unit(1, 0, 0, before=do((have_near, 1)), after=do((landed, 2, 1)))
        + unit(1, 0, 1, before=exchange_q(1).wait_recv, after=do((second, 1, 0)))
        + unit(0, 1, 0, mid=do((landed, 2, 2)), after=do((second, 1, 1)))
    )
    w_cp.start()
    have_far(1)
    tiles(
        unit(1, 1, 1, after=do((hand_over, 1, 0), (hand_over, 1, 1)))
        + unit(2, 0, 0, before=do((have_near, 2)), after=do((second, 2, 0)))
        + unit(2, 0, 1, before=exchange_q(2).wait_recv, after=do((second, 2, 1)))
        + unit(1, 1, 0, after=do((merge, 0, 0), (merge, 0, 1)))
    )
    have_far(2)
    tiles(
        [(2, 1, OWN + part_span(p)[0], part_span(p)[1], None, do((hand_over, 2, p))) for p in range(2)]
        + [(2, 1, *part_span(p), None, None) for p in range(2)]
    )
    wait_bytes(w_got, w_recv.at[0])
    w_fwd.start()
    merge(1, 0)
    merge(2, 0)
    merge(1, 1)
    merge(2, 1)

    S = ((SB0, SC0), (SB1, SC1))
    R = ((RB0, RC0), (RB1, RC1))

    def scatter(p, k, n, i):
        cols = pl.ds(n * CH, CH)
        count = PARTS[p][1]
        to = lax.rem((x, z)[k] + i, 4)
        return remote(
            S[p][k].at[pl.ds(pl.multiple_of(to * count, 16), count), cols], R[p][k].at[i - 1, :, cols],
            r_send.at[p, k, n, i - 1], r_recv.at[p, k, n], dev(to, y, z, c) if k == 0 else dev(x, y, to, c),
        )

    for cp in w_loc:
        cp.wait()
    wait_bytes(w_sib, w_recv.at[1])
    step = ts[0]
    for p in range(2):
        first, count = PARTS[p]
        wait_bytes(OG[p].at[0], g_recv.at[p, 0])
        wait_bytes(OG[p].at[1], g_recv.at[p, 1])
        hidden = jnp.concatenate([HID[pl.ds(q * 48 + first, count)] for q in range(4)], axis=0).astype(jnp.float32)
        for n in range(3072 // CH):
            cols = pl.ds(n * CH, CH)
            got = jnp.dot(OG[p][0], WX[:, cols], preferred_element_type=jnp.float32)
            S[p][0][:, cols] = (GT[step, 0:1, cols] * got).astype(jnp.bfloat16)
            for i in range(1, 4):
                scatter(p, 0, n, i).start()
            got = GT[step, 1:2, cols] * jnp.dot(OG[p][1], WC[:, cols], preferred_element_type=jnp.float32)
            got = got + jnp.where(z == n, hidden, 0.0)
            S[p][1][:, cols] = (gain[0:1, cols] * got).astype(jnp.bfloat16)
            for i in range(1, 4):
                scatter(p, 1, n, i).start()
    for p in range(2):
        first, count = PARTS[p]
        for n in range(3072 // CH):
            cols = pl.ds(n * CH, CH)
            total = bh[0, pl.ds(first, count), cols].astype(jnp.float32)
            for k in range(2):
                wait_bytes(R[p][k].at[:, :, cols], r_recv.at[p, k, n])
                own = pl.ds(pl.multiple_of((x, z)[k] * count, 16), count)
                total = total + S[p][k][own, cols].astype(jnp.float32)
                for i in range(3):
                    total = total + R[p][k][i, :, cols].astype(jnp.float32)
            out[pl.ds(first, count), cols] = total.astype(jnp.bfloat16)

    for h in range(NH):
        for a in range(3):
            @pl.when(yh == 0)
            def _():
                wait_bytes(K.at[h, pl.ds(0, 7 * 48)], s1_base.at[a, h])
                wait_bytes(K.at[h, pl.ds(0, 384)], s1_ctl.at[a, h])

            @pl.when(yh == 1)
            def _():
                wait_bytes(K.at[h, pl.ds(0, 8 * 48)], s1_base.at[a, h])
                wait_bytes(K.at[h, pl.ds(0, 192)], s1_ctl.at[a, h])
        for i in range(2):
            for k in range(3):
                exchange(i, h, k).wait_send()
        exchange_q(h).wait_send()
        for p in range(2):
            for cp in send_part(h, p):
                cp.wait_send()
            for i in range(1, 4):
                give(h, p, i).wait_send()
    w_cp.wait_send()
    w_fwd.wait_send()
    for n in range(3072 // CH):
        for p in range(2):
            for k in range(2):
                for i in range(1, 4):
                    scatter(p, k, n, i).wait_send()


def per_device(
    base_hidden, base_query, base_key, base_value, base_text_key, base_text_value, base_out_weight,
    control_hidden, control_query, control_key, control_value, control_text_key, control_text_value,
    control_out_weight, gate_table, control_gain, timestep, text_length,
):
    bf, f32 = jnp.bfloat16, jnp.float32
    vm, hbm = pl.BlockSpec(memory_space=pltpu.VMEM), pl.BlockSpec(memory_space=pl.ANY)
    dma = pltpu.SemaphoreType.DMA
    out = pl.pallas_call(
        kernel,
        out_shape=jax.ShapeDtypeStruct((48, 3072), bf),
        in_specs=[pl.BlockSpec(memory_space=pltpu.SMEM)] * 2 + [vm] + [hbm] * 14 + [vm],
        out_specs=vm,
        scratch_shapes=[
            pltpu.VMEM((NH, 2 * OWN, HD), bf),
            pltpu.VMEM((NH, KALL, HD), bf),
            pltpu.VMEM((NH, KALL, HD), bf),
            pltpu.VMEM((NH, 2 * OWN, HD), f32),
            pltpu.VMEM((NH, 2 * OWN, HD), f32),
            pltpu.VMEM((NH, 2 * OWN, HD), f32),
            pltpu.VMEM((NH, OWN, HD), bf),
            pltpu.VMEM((NH, 2, 8, HD), f32),
            pltpu.VMEM((NH, OWN, HD), bf),
            pltpu.VMEM((NH, 2, 8, HD), f32),
            pltpu.VMEM((NH, OWN, HD), bf),
            pltpu.VMEM((2, 64, 768), bf),
            pltpu.VMEM((2, 128, 768), bf),
            pltpu.VMEM((768, 3072), bf),
            pltpu.VMEM((768, 3072), bf),
            pltpu.VMEM((192, 768), bf),
            pltpu.VMEM((28, 2, 3072), f32),
            pltpu.VMEM((64, 3072), bf),
            pltpu.VMEM((128, 3072), bf),
            pltpu.VMEM((64, 3072), bf),
            pltpu.VMEM((128, 3072), bf),
            pltpu.VMEM((3, 16, 3072), bf),
            pltpu.VMEM((3, 32, 3072), bf),
            pltpu.VMEM((3, 16, 3072), bf),
            pltpu.VMEM((3, 32, 3072), bf),
            dma((3, NH)), dma((3, NH)), dma((3, NH)),
            dma((2, NH, 3)), dma((2, NH, 3)), dma((NH,)), dma((NH,)),
            dma((2, NH, 2)), dma((2, NH, 2)), dma((NH, 2, 4)), dma((2, 2)),
            dma((2,)), dma((2,)), dma((2, 2, 4, 3)), dma((2, 2, 4)), dma((10,)),
        ],
        compiler_params=pltpu.CompilerParams(
            collective_id=0, has_side_effects=True, vmem_limit_bytes=56 * 2**20
        ),
        cost_estimate=pl.CostEstimate(flops=10**10, bytes_accessed=3 * 10**7, transcendentals=16 * 10**6),
    )(
        text_length, timestep, base_hidden, base_query, base_key, base_value, base_text_key, base_text_value,
        base_out_weight, control_hidden, control_query, control_key, control_value, control_text_key,
        control_text_value, control_out_weight, gate_table, control_gain.reshape(1, -1),
    )
    return out.reshape(1, 48, 3072)


def solution(mesh):
    rows, cols = P(("seq", "rep"), "grp", None), P(("seq", "rep"), "grp")
    placed = (
        rows, rows, rows, rows, P(None, "seq"), P(None, "seq"), P("seq", None),
        cols, cols, cols, cols, P(None, "grp"), P(None, "grp"), P("grp", None),
        P(), P(), P(), P(),
    )
    return jax.shard_map(per_device, mesh=mesh, in_specs=placed, out_specs=rows, check_vma=False)
```

```python
import math

import jax
import jax.numpy as jnp
from jax import lax
from jax.experimental import pallas as pl
from jax.experimental.pallas import tpu as pltpu
from jax.sharding import PartitionSpec as P

HD = 128
NH = 3
OWN = 768
TXH = 256
KA = TXH + 2 * OWN
KALL = TXH + 4 * OWN
ROWS = 384
PARTS = ((0, 16), (16, 32))
CH = 768
C2 = math.log2(math.e) / math.sqrt(HD)
BLOCK = ((0, KA), (KA, 2 * OWN))
FAR_FIRST = (2, 1, 3)
NT = (((1,), (1,)), ((), ()))
MESH = pl.DeviceIdType.MESH


def remote(src, dst, ssem, rsem, dev):
    return pltpu.make_async_remote_copy(
        src_ref=src, dst_ref=dst, send_sem=ssem, recv_sem=rsem, device_id=dev, device_id_type=MESH
    )


def wait_bytes(ref, sem):
    pltpu.make_async_copy(ref, ref, sem).wait()


def kernel(
    tl, ts, bh, bq, bk, bv, btk, btv, wb, ch, cq, ck, cv, ctk, ctv, wc, table, gain, out,
    Q, K, V, M, L, A, PO, PS, RO, RS, O, OG0, OG1, WX, WC, HID, GT, SB0, SB1, SC0, SC1, RB0, RB1, RC0, RC1,
    s1_recv, s1_base, s1_ctl, ex_send, ex_recv, q_send, q_recv, p_send, p_recv,
    g_send, g_recv, w_send, w_recv, r_send, r_recv, loc,
):
    z = lax.axis_index("grp")
    seq = lax.axis_index("seq")
    rep = lax.axis_index("rep")
    x, yl = lax.rem(seq, 4), seq // 4
    yh, c = rep // 2, lax.rem(rep, 2)
    y = yh * 2 + yl

    def dev(xx, yy, zz, cc):
        return {"grp": zz, "seq": lax.rem(yy, 2) * 4 + xx, "rep": (yy // 2) * 2 + cc}

    sib = dev(x, y, z, 1 - c)
    pos = (1 - yh) * z + yh * x
    pa = pos + 1 - 2 * lax.rem(pos, 2)
    pb = lax.rem(pos + 3 - 2 * lax.rem(pos, 2), 4)
    dev_a = dev(yh * pa + (1 - yh) * x, y, (1 - yh) * pa + yh * z, c)
    dev_b = dev(yh * pb + (1 - yh) * x, y, (1 - yh) * pb + yh * z, c)
    kv_dev, q_dev = (dev_a, dev_a, dev_b), (dev_b, dev_b, dev_a)
    thalf = (pos // 2, pos // 2, lax.rem(pos + 1, 4) // 2)

    w_loc = [
        pltpu.make_async_copy(wc, WC, loc.at[0]),
        pltpu.make_async_copy(wb, WX.at[pl.ds(pl.multiple_of(yl * 384, 128), 384)], loc.at[1]),
        pltpu.make_async_copy(ch, HID, loc.at[2]),
        pltpu.make_async_copy(table, GT, loc.at[9]),
    ]

    def text_copies(h, is_base):
        rows = pl.ds(pl.multiple_of(thalf[h] * TXH, TXH), TXH)
        if is_base:
            cols = pl.ds(h * HD, HD)
            srcs = (btk, btv)
        else:
            cols = pl.ds(pl.multiple_of(yl * 384 + h * HD, HD), HD)
            srcs = (ctk, ctv)
        return [
            pltpu.make_async_copy(srcs[i].at[rows, cols], (K, V)[i].at[h, pl.ds(0, TXH)], loc.at[3 + i * NH + h])
            for i in range(2)
        ]

    @pl.when(yh == 0)
    def _():
        for h in range(NH):
            for cp in text_copies(h, True):
                cp.start()

    @pl.when(yh == 1)
    def _():
        for h in range(NH):
            for cp in text_copies(h, False):
                cp.start()

    barrier = pltpu.get_barrier_semaphore()
    peers = [dev(lax.rem(x + i % 4, 4), lax.rem(y + i // 4, 4), z, c) for i in range(1, 16)]
    peers += [dev(x, y, lax.rem(z + i, 4), c) for i in range(1, 4)] + [sib]
    for d in peers:
        pl.semaphore_signal(barrier, inc=1, device_id=d, device_id_type=MESH)
    pl.semaphore_wait(barrier, len(peers))

    base_rows = pl.multiple_of((y * 4 + x) * 48, 16)
    ctl_rows = pl.multiple_of(y * 192, 16)
    arrays = ((bk, ck, K, TXH), (bq, cq, Q, 0), (bv, cv, V, TXH))
    def part_rows(p, block):
        first, count = PARTS[p]
        return pl.ds(pl.multiple_of(first * 16 + block * count, 16), count)

    def stage1(h, a):
        bsrc, csrc, dst, off = arrays[a]
        sem = s1_recv.at[a, h]
        for i in range(2):
            b = lax.rem(yl + i, 2)
            cols = pl.ds(pl.multiple_of(b * 384 + h * HD, HD), HD)
            if a == 1:
                pieces = [
                    (csrc.at[pl.ds(q * 48 + PARTS[p][0], PARTS[p][1]), cols], dst.at[h, part_rows(p, y * 4 + q)])
                    for q in range(4) for p in range(2)
                ]
            else:
                pieces = [(csrc.at[:, cols], dst.at[h, pl.ds(off + ctl_rows, 192)])]
            for src, to in pieces:
                cp = remote(src, to, s1_ctl.at[a, h], sem, {"grp": z, "seq": b * 4 + x, "rep": 2 + c})
                if i:
                    cp.start()
                else:
                    pl.when(yh == 0)(cp.start)
                    pl.when(yh == 1)(pltpu.make_async_copy(src, to, sem).start)
        for i in range(8):
            s = lax.rem(seq + i, 8)
            cols = pl.ds(pl.multiple_of(s * 384 + h * HD, HD), HD)
            if a == 1:
                pieces = [
                    (bsrc.at[0, pl.ds(*PARTS[p]), cols], dst.at[h, part_rows(p, y * 4 + x)]) for p in range(2)
                ]
            else:
                pieces = [(bsrc.at[0, :, cols], dst.at[h, pl.ds(off + base_rows, 48)])]
            for src, to in pieces:
                cp = remote(src, to, s1_base.at[a, h], sem, {"grp": z, "seq": s, "rep": c})
                if i:
                    cp.start()
                else:
                    pl.when(yh == 1)(cp.start)
                    pl.when(yh == 0)(pltpu.make_async_copy(src, to, sem).start)

    for a in range(3):
        stage1(0, a)
    for cp in w_loc:
        cp.start()

    kv = ((0, K), (2, V))

    def exchange(i, h, k):
        buf = kv[i][1]
        lo = TXH + (0, 0, 2 * OWN)[k]
        to = TXH + (OWN, 2 * OWN, 3 * OWN)[k]
        return remote(
            buf.at[h, pl.ds(lo, OWN)], buf.at[h, pl.ds(to, OWN)],
            ex_send.at[i, h, k], ex_recv.at[i, h, k], (sib, kv_dev[h], sib)[k],
        )

    def exchange_q(h):
        return remote(Q.at[h, pl.ds(0, OWN)], Q.at[h, pl.ds(OWN, OWN)], q_send.at[h], q_recv.at[h], q_dev[h])

    def landed(h, a):
        dst, off = arrays[a][2:]
        wait_bytes(dst.at[h, pl.ds(off, OWN)], s1_recv.at[a, h])
        if a == 0 and h + 1 < NH:
            for i in range(3):
                stage1(h + 1, i)
        if a == 1:
            exchange_q(h).start()
        else:
            exchange(a // 2, h, 1).start()
            exchange(a // 2, h, 0).start()

    def second(h, i):
        exchange(i, h, 1).wait_recv()
        exchange(i, h, 2).start()

    text_at = lax.broadcasted_iota(jnp.int32, (ROWS, TXH), 1)

    def scores(h, r, size, lo, n):
        s = lax.dot_general(
            Q[h, pl.ds(r, size)], K[h, pl.ds(lo, n)], NT, preferred_element_type=jnp.float32
        )
        if lo == 0:
            s = jnp.concatenate([jnp.where(text_at + thalf[h] * TXH < tl[0], s[:, :TXH], -1e30), s[:, TXH:]], axis=1)
        return s

    def fold(h, r, size, s, lo, n):
        rows = pl.ds(r, size)
        top = jnp.broadcast_to(jnp.max(s, axis=1, keepdims=True), (size, HD))
        if lo:
            old = M[h, rows]
            top = jnp.maximum(old, top)
            f = jnp.exp2((old - top) * C2)
        M[h, rows] = top
        w = jnp.exp2((s - top[:, :1]) * C2)
        part = w[:, :HD]
        for i in range(1, n // HD):
            part = part + w[:, i * HD:(i + 1) * HD]
        got = jnp.dot(w.astype(jnp.bfloat16), V[h, pl.ds(lo, n)], preferred_element_type=jnp.float32)
        if lo:
            L[h, rows] = L[h, rows] * f + part
            A[h, rows] = A[h, rows] * f + got
        else:
            L[h, rows] = part
            A[h, rows] = got

    def tiles(todo):
        def first(item):
            h, b, r, size, before, _ = item
            if before is not None:
                before()
            return scores(h, r, size, *BLOCK[b])

        s = first(todo[0])
        for i, (h, b, r, size, _, after) in enumerate(todo):
            later = first(todo[i + 1]) if i + 1 < len(todo) else None
            fold(h, r, size, s, *BLOCK[b])
            if after is not None:
                after()
            s = later

    def part_span(p):
        return PARTS[p][0] * 16, PARTS[p][1] * 16

    def send_part(h, p):
        rows = pl.ds(*part_span(p))
        return [
            remote(PO.at[h, rows], RO.at[h, rows], p_send.at[0, h, p], p_recv.at[0, h, p], q_dev[h]),
            remote(PS.at[h, p], RS.at[h, p], p_send.at[1, h, p], p_recv.at[1, h, p], q_dev[h]),
        ]

    eye = lax.broadcasted_iota(jnp.int32, (HD, HD), 0) == lax.broadcasted_iota(jnp.int32, (HD, HD), 1)

    def log_sum(h, rows):
        total = jnp.broadcast_to(jnp.sum(L[h, rows], axis=1, keepdims=True), (HD, HD))
        return total, M[h, rows] * C2 + jnp.log2(total)

    def hand_over(h, p):
        first, count = part_span(p)
        for i in range(count // HD):
            rows = pl.ds(OWN + first + i * HD, HD)
            total, both = log_sum(h, rows)
            PO[h, pl.ds(first + i * HD, HD)] = (A[h, rows] / total).astype(jnp.bfloat16)
            PS[h, p, pl.ds(i, 1)] = jnp.sum(jnp.where(eye, both, 0.0), axis=0, keepdims=True)
        for i in range(count // HD, 8):
            PS[h, p, pl.ds(i, 1)] = jnp.zeros((1, HD), jnp.float32)
        for cp in send_part(h, p):
            cp.start()

    def have_near(h):
        for i in range(2):
            exchange(i, h, 0).wait_recv()
            wait_bytes((K, V)[i].at[h, pl.ds(0, TXH)], loc.at[3 + i * NH + h])

    def have_far(h):
        for i in range(2):
            exchange(i, h, 2).wait_recv()

    def unit(h, b, far, before=None, mid=None, after=None):
        r = far * OWN
        return [(h, b, r, ROWS, before, mid), (h, b, r + ROWS, ROWS, None, after)]

    def do(*steps):
        def run():
            for f, *args in steps:
                f(*args)
        return run

    OG = (OG0, OG1)

    def give(h, p, i):
        to = lax.rem(y + i, 4)
        first, count = PARTS[p]
        src = O.at[h, pl.ds(pl.multiple_of(first * 16 + to * 4 * count, 16), 4 * count)]
        dst = OG[p].at[yh, :, pl.ds(pl.multiple_of(yl * 384 + h * HD, HD), HD)]
        if i == 0:
            return pltpu.make_async_copy(src, dst, g_recv.at[p, yh])
        return remote(src, dst, g_send.at[h, p, i], g_recv.at[p, yh], dev(x, to, z, c))

    def merge(h, p):
        for cp in send_part(h, p):
            cp.wait_recv()
        first, count = part_span(p)
        for i in range(count // HD):
            rows = pl.ds(first + i * HD, HD)
            total, mine = log_sum(h, rows)
            theirs = jnp.sum(jnp.where(eye, RS[h, p, pl.ds(i, 1)], 0.0), axis=1, keepdims=True)
            theirs = jnp.broadcast_to(theirs, (HD, HD))
            top = jnp.maximum(mine, theirs)
            u, v = jnp.exp2(mine - top), jnp.exp2(theirs - top)
            value = A[h, rows] * (u / total) + RO[h, rows].astype(jnp.float32) * v
            O[h, rows] = (value / (u + v)).astype(jnp.bfloat16)
        for i in (*FAR_FIRST, 0):
            give(h, p, i).start()

    w_half = pl.ds(pl.multiple_of(c * 192, 16), 192)
    w_cp = remote(
        wb.at[w_half], WX.at[pl.ds(pl.multiple_of(yl * 384 + c * 192, 16), 192)],
        w_send.at[0], w_recv.at[0], dev(x, lax.rem(y + 3 + 2 * c, 4), z, c),
    )
    w_got = WX.at[pl.ds(pl.multiple_of((1 - yl) * 384 + c * 192, 16), 192)]
    w_sib = WX.at[pl.ds(pl.multiple_of((1 - yl) * 384 + (1 - c) * 192, 16), 192)]
    w_fwd = remote(w_got, w_got, w_send.at[1], w_recv.at[1], sib)

    landed(0, 0)
    landed(0, 1)
    landed(0, 2)
    have_near(0)
    tiles(unit(0, 0, 0, mid=do((landed, 1, 0)), after=do((second, 0, 0))))
    exchange_q(0).wait_recv()
    tiles(unit(0, 0, 1, mid=do((landed, 1, 1)), after=do((second, 0, 1), (landed, 1, 2))))
    have_far(0)
    tiles(
        unit(0, 1, 1, after=do((hand_over, 0, 0), (hand_over, 0, 1), (landed, 2, 0)))
        + unit(1, 0, 0, before=do((have_near, 1)), after=do((landed, 2, 1)))
        + unit(1, 0, 1, before=exchange_q(1).wait_recv, after=do((second, 1, 0)))
        + unit(0, 1, 0, mid=do((landed, 2, 2)), after=do((second, 1, 1)))
    )
    w_cp.start()
    have_far(1)
    tiles(
        unit(1, 1, 1, after=do((hand_over, 1, 0), (hand_over, 1, 1)))
        + unit(2, 0, 0, before=do((have_near, 2)), after=do((second, 2, 0)))
        + unit(2, 0, 1, before=exchange_q(2).wait_recv, after=do((second, 2, 1)))
        + unit(1, 1, 0, after=do((merge, 0, 0), (merge, 0, 1)))
    )
    have_far(2)
    tiles(
        [(2, 1, OWN + part_span(p)[0], part_span(p)[1], None, do((hand_over, 2, p))) for p in range(2)]
        + [(2, 1, *part_span(p), None, None) for p in range(2)]
    )
    wait_bytes(w_got, w_recv.at[0])
    w_fwd.start()
    merge(1, 0)
    merge(2, 0)
    merge(1, 1)
    merge(2, 1)

    S = ((SB0, SC0), (SB1, SC1))
    R = ((RB0, RC0), (RB1, RC1))

    def scatter(p, k, n, i):
        cols = pl.ds(n * CH, CH)
        count = PARTS[p][1]
        to = lax.rem((x, z)[k] + i, 4)
        return remote(
            S[p][k].at[pl.ds(pl.multiple_of(to * count, 16), count), cols], R[p][k].at[i - 1, :, cols],
            r_send.at[p, k, n, i - 1], r_recv.at[p, k, n], dev(to, y, z, c) if k == 0 else dev(x, y, to, c),
        )

    for cp in w_loc:
        cp.wait()
    wait_bytes(w_sib, w_recv.at[1])
    step = ts[0]
    for p in range(2):
        first, count = PARTS[p]
        wait_bytes(OG[p].at[0], g_recv.at[p, 0])
        wait_bytes(OG[p].at[1], g_recv.at[p, 1])
        hidden = jnp.concatenate([HID[pl.ds(q * 48 + first, count)] for q in range(4)], axis=0).astype(jnp.float32)
        for n in range(3072 // CH):
            cols = pl.ds(n * CH, CH)
            got = jnp.dot(OG[p][0], WX[:, cols], preferred_element_type=jnp.float32)
            S[p][0][:, cols] = (GT[step, 0:1, cols] * got).astype(jnp.bfloat16)
            for i in FAR_FIRST:
                scatter(p, 0, n, i).start()
            got = GT[step, 1:2, cols] * jnp.dot(OG[p][1], WC[:, cols], preferred_element_type=jnp.float32)
            got = got + jnp.where(z == n, hidden, 0.0)
            S[p][1][:, cols] = (gain[0:1, cols] * got).astype(jnp.bfloat16)
            for i in FAR_FIRST:
                scatter(p, 1, n, i).start()
    for p in range(2):
        first, count = PARTS[p]
        for n in range(3072 // CH):
            cols = pl.ds(n * CH, CH)
            total = bh[0, pl.ds(first, count), cols].astype(jnp.float32)
            for k in range(2):
                wait_bytes(R[p][k].at[:, :, cols], r_recv.at[p, k, n])
                own = pl.ds(pl.multiple_of((x, z)[k] * count, 16), count)
                total = total + S[p][k][own, cols].astype(jnp.float32)
                for i in range(3):
                    total = total + R[p][k][i, :, cols].astype(jnp.float32)
            out[pl.ds(first, count), cols] = total.astype(jnp.bfloat16)

    for h in range(NH):
        for a in range(3):
            @pl.when(yh == 0)
            def _():
                wait_bytes(K.at[h, pl.ds(0, 7 * 48)], s1_base.at[a, h])
                wait_bytes(K.at[h, pl.ds(0, 384)], s1_ctl.at[a, h])

            @pl.when(yh == 1)
            def _():
                wait_bytes(K.at[h, pl.ds(0, 8 * 48)], s1_base.at[a, h])
                wait_bytes(K.at[h, pl.ds(0, 192)], s1_ctl.at[a, h])
        for i in range(2):
            for k in range(3):
                exchange(i, h, k).wait_send()
        exchange_q(h).wait_send()
        for p in range(2):
            for cp in send_part(h, p):
                cp.wait_send()
            for i in range(1, 4):
                give(h, p, i).wait_send()
    w_cp.wait_send()
    w_fwd.wait_send()
    for n in range(3072 // CH):
        for p in range(2):
            for k in range(2):
                for i in range(1, 4):
                    scatter(p, k, n, i).wait_send()


def per_device(
    base_hidden, base_query, base_key, base_value, base_text_key, base_text_value, base_out_weight,
    control_hidden, control_query, control_key, control_value, control_text_key, control_text_value,
    control_out_weight, gate_table, control_gain, timestep, text_length,
):
    bf, f32 = jnp.bfloat16, jnp.float32
    vm, hbm = pl.BlockSpec(memory_space=pltpu.VMEM), pl.BlockSpec(memory_space=pl.ANY)
    dma = pltpu.SemaphoreType.DMA
    out = pl.pallas_call(
        kernel,
        out_shape=jax.ShapeDtypeStruct((48, 3072), bf),
        in_specs=[pl.BlockSpec(memory_space=pltpu.SMEM)] * 2 + [vm] + [hbm] * 14 + [vm],
        out_specs=vm,
        scratch_shapes=[
            pltpu.VMEM((NH, 2 * OWN, HD), bf),
            pltpu.VMEM((NH, KALL, HD), bf),
            pltpu.VMEM((NH, KALL, HD), bf),
            pltpu.VMEM((NH, 2 * OWN, HD), f32),
            pltpu.VMEM((NH, 2 * OWN, HD), f32),
            pltpu.VMEM((NH, 2 * OWN, HD), f32),
            pltpu.VMEM((NH, OWN, HD), bf),
            pltpu.VMEM((NH, 2, 8, HD), f32),
            pltpu.VMEM((NH, OWN, HD), bf),
            pltpu.VMEM((NH, 2, 8, HD), f32),
            pltpu.VMEM((NH, OWN, HD), bf),
            pltpu.VMEM((2, 64, 768), bf),
            pltpu.VMEM((2, 128, 768), bf),
            pltpu.VMEM((768, 3072), bf),
            pltpu.VMEM((768, 3072), bf),
            pltpu.VMEM((192, 768), bf),
            pltpu.VMEM((28, 2, 3072), f32),
            pltpu.VMEM((64, 3072), bf),
            pltpu.VMEM((128, 3072), bf),
            pltpu.VMEM((64, 3072), bf),
            pltpu.VMEM((128, 3072), bf),
            pltpu.VMEM((3, 16, 3072), bf),
            pltpu.VMEM((3, 32, 3072), bf),
            pltpu.VMEM((3, 16, 3072), bf),
            pltpu.VMEM((3, 32, 3072), bf),
            dma((3, NH)), dma((3, NH)), dma((3, NH)),
            dma((2, NH, 3)), dma((2, NH, 3)), dma((NH,)), dma((NH,)),
            dma((2, NH, 2)), dma((2, NH, 2)), dma((NH, 2, 4)), dma((2, 2)),
            dma((2,)), dma((2,)), dma((2, 2, 4, 3)), dma((2, 2, 4)), dma((10,)),
        ],
        compiler_params=pltpu.CompilerParams(
            collective_id=0, has_side_effects=True, vmem_limit_bytes=56 * 2**20
        ),
        cost_estimate=pl.CostEstimate(flops=10**10, bytes_accessed=3 * 10**7, transcendentals=16 * 10**6),
    )(
        text_length, timestep, base_hidden, base_query, base_key, base_value, base_text_key, base_text_value,
        base_out_weight, control_hidden, control_query, control_key, control_value, control_text_key,
        control_text_value, control_out_weight, gate_table, control_gain.reshape(1, -1),
    )
    return out.reshape(1, 48, 3072)


def solution(mesh):
    rows, cols = P(("seq", "rep"), "grp", None), P(("seq", "rep"), "grp")
    placed = (
        rows, rows, rows, rows, P(None, "seq"), P(None, "seq"), P("seq", None),
        cols, cols, cols, cols, P(None, "grp"), P(None, "grp"), P("grp", None),
        P(), P(), P(), P(),
    )
    return jax.shard_map(per_device, mesh=mesh, in_specs=placed, out_specs=rows, check_vma=False)
```
